32 devices in a mesh: span: 8 (over y, x, core), tok: 4 (over z).
Axes of the slice: x: 2, y: 2, z: 4, core: 2. Of those that a mesh axis runs over, the one named last changes fastest.
Arguments:
- tokens: bfloat16 [16384, 256], P(('span', 'tok')), may hold values from -6 to 6
- w_in: bfloat16 [256, 768], replicated, may hold values from -0.375 to 0.375
- short_filter: float32 [3, 768], replicated, may hold values from -3 to 3
- long_filter: bfloat16 [256, 8192], P('tok'), may hold values from -0.0625 to 0.0625
- skip_gain: float32 [256], P('tok'), may hold values from 0.5 to 1.5
- w_out: bfloat16 [256, 256], replicated, may hold values from -0.375 to 0.375
Outputs:
- output: bfloat16 [16384, 256], P(('span', 'tok'))
The draws below stay inside these ranges and needn't reach their ends.
All inputs are finite; a program needn't handle non-finite values.
Results may differ from the reference program's by a relative error of at most 0.0081.
Values may be sent and summed in bfloat16 or wider, within the bound.
A program may use at most 64 MiB of HBM per device.

```python
import jax
import jax.numpy as jnp
from jax import lax

D = 256
FILT = 8192
SEQ = 16384


def shard_levels(own_key, extent, pieces, least, top_value):
    gain = 1.0
    for axis_at, blocks in pieces:
        heights = jax.random.uniform(jax.random.fold_in(jax.random.fold_in(own_key, 6), axis_at), (blocks,), jnp.float32, least / len(pieces), top_value / len(pieces))
        gain = gain * jnp.repeat(jnp.exp(heights), extent[axis_at] // blocks).reshape((-1,) + (1,) * (len(extent) - 1 - axis_at))
    return gain


def scatter_about(stream_key, dims, width, most, split=(), dtype=jnp.bfloat16):
    level = shard_levels(stream_key, dims, split, -0.22, 0.18) if split else 1.0
    drawn = jax.random.normal(stream_key, dims, jnp.float32) * width * level
    return jnp.minimum(jnp.maximum(drawn, -most), most).astype(dtype)


def setup_inputs(seed: int = 0) -> dict:
    arg_keys = jax.random.split(jax.random.key(seed), 7)
    tokens = scatter_about(arg_keys[0], (SEQ, D), 1.0, 6.0, ((0, 32),))
    w_in = scatter_about(arg_keys[1], (D, 3 * D), D ** -0.5, 0.375)
    short_filter = scatter_about(arg_keys[2], (3, 3 * D), 0.6, 3.0, (), jnp.float32)
    long_filter = scatter_about(arg_keys[3], (D, FILT), FILT ** -0.5, 0.0625, ((0, 4),))
    skip_gain = jnp.clip(0.5 + 1.0 * jax.random.uniform(arg_keys[4], (D,), jnp.float32) ** shard_levels(arg_keys[4], (D,), ((0, 4),), -0.2, 0.2), 0.5, 1.5)
    w_out = scatter_about(arg_keys[5], (D, D), D ** -0.5, 0.375)
    return {"tokens": tokens, "w_in": w_in, "short_filter": short_filter, "long_filter": long_filter, "skip_gain": skip_gain, "w_out": w_out}


def reference(tokens, w_in, short_filter, long_filter, skip_gain, w_out):
    projected = jnp.dot(tokens, w_in, preferred_element_type=jnp.float32).astype(jnp.bfloat16)
    projected = lax.optimization_barrier(projected).astype(jnp.float32)
    padded = jnp.pad(projected, ((2, 0), (0, 0)))
    mixed = short_filter[0] * padded[2:] + short_filter[1] * padded[1:-1] + short_filter[2] * padded[:-2]
    query_rows = mixed[:, :D]
    key_rows = mixed[:, D:2 * D]
    value_rows = mixed[:, 2 * D:]
    product = (key_rows * value_rows).astype(jnp.bfloat16)
    total = product.shape[0]
    taps_count = long_filter.shape[1]
    fft_len = 1
    while fft_len < total + taps_count:
        fft_len = fft_len * 2
    product_f = lax.optimization_barrier(product).astype(jnp.float32)
    spectrum = jnp.fft.rfft(product_f, n=fft_len, axis=0) * jnp.fft.rfft(long_filter.astype(jnp.float32).T, n=fft_len, axis=0)
    conv_full = jnp.fft.irfft(spectrum, n=fft_len, axis=0)[:total].astype(jnp.float32)
    convolved = (conv_full + skip_gain * product_f).astype(jnp.bfloat16)
    convolved = lax.optimization_barrier(convolved).astype(jnp.float32)
    gated = (query_rows * convolved).astype(jnp.bfloat16)
    return jnp.dot(gated, w_out, preferred_element_type=jnp.float32).astype(jnp.bfloat16)
```

```python
import functools

import jax
import jax.numpy as jnp
from jax import lax
from jax.experimental import pallas as pl
from jax.experimental.pallas import tpu as pltpu
from jax.sharding import PartitionSpec as P

D = 256
LANES = 128
GROUP = 8


def build_toeplitz(row_of, blocks, toeplitz_ref):
    row_at = lax.broadcasted_iota(jnp.int32, (LANES, LANES), 0)
    col_at = lax.broadcasted_iota(jnp.int32, (LANES, LANES), 1)
    upper = col_at >= row_at

    def step(b, before):
        spread = jnp.broadcast_to(row_of(b), (LANES, LANES))
        turned = pltpu.roll(spread, 0, 1, stride=1, stride_axis=0)
        toeplitz_ref[pl.ds(pl.multiple_of(b * LANES, LANES), LANES), :] = jnp.where(
            upper, turned, before
        ).astype(jnp.bfloat16)
        return turned

    last = lax.fori_loop(0, blocks, step, jnp.zeros((LANES, LANES), jnp.float32))
    toeplitz_ref[blocks * LANES :, :] = jnp.where(upper, 0.0, last).astype(jnp.bfloat16)


def lagged(padded_ref, parts, rows, reach, lags):
    columns = []
    for b in lags:
        pieces = []
        for m in range(parts):
            back, part = divmod(m - b, parts)
            pieces.append(padded_ref[part, pl.ds(reach + back, rows), :])
        columns.append(jnp.concatenate(pieces, axis=0).astype(jnp.bfloat16))
    return jnp.concatenate(columns, axis=1) if len(columns) > 1 else columns[0]


def conv_channel(padded_ref, toeplitz_ref, parts, rows, reach, blocks):
    total = jnp.zeros((parts * rows, LANES), jnp.float32)
    for start in range(0, blocks + 1, GROUP):
        lags = range(start, min(start + GROUP, blocks + 1))
        total = total + jnp.dot(
            lagged(padded_ref, parts, rows, reach, lags),
            toeplitz_ref[start * LANES : (lags[-1] + 1) * LANES, :],
            preferred_element_type=jnp.float32,
        )
    return total


def conv_kernel(parts, rows, reach, blocks, gain_ref, x_ref, h_ref, y_ref, padded_ref, toeplitz_ref):
    build_toeplitz(lambda b: h_ref[0, pl.ds(b, 1), :], blocks, toeplitz_ref)
    padded_ref[:, :reach, :] = jnp.zeros((parts, reach, LANES), jnp.float32)
    padded_ref[:, reach:, :] = x_ref[0].astype(jnp.float32)
    total = conv_channel(padded_ref, toeplitz_ref, parts, rows, reach, blocks)
    gain = gain_ref[pl.program_id(0)]
    for m in range(parts):
        y_ref[0, m] = (total[m * rows : (m + 1) * rows] + gain * padded_ref[m, reach:, :]).astype(
            jnp.bfloat16
        )


def per_device(tokens, w_in, short_filter, long_filter, skip_gain, w_out):
    tok_rows = tokens.shape[0]
    spans, toks = lax.axis_size("span"), lax.axis_size("tok")
    peers = spans * toks
    parts = tok_rows // LANES
    taps_count = long_filter.shape[1]
    blocks = taps_count // LANES
    reach = -(-taps_count // tok_rows)
    chans = long_filter.shape[0] // spans
    pairs = [(i, i + 1) for i in range(peers - 1)]
    rim = lax.ppermute(tokens[tok_rows - 2 :], ("span", "tok"), pairs)
    projected = lax.dot_general(
        w_in,
        jnp.concatenate([rim, tokens], axis=0),
        (((0,), (1,)), ((), ())),
        preferred_element_type=jnp.float32,
    ).astype(jnp.bfloat16)
    padded = lax.optimization_barrier(projected).astype(jnp.float32)
    mixed = (
        short_filter[0][:, None] * padded[:, 2:]
        + short_filter[1][:, None] * padded[:, 1:-1]
        + short_filter[2][:, None] * padded[:, :-2]
    )
    query_rows = mixed[:D]
    product = (mixed[D : 2 * D] * mixed[2 * D :]).astype(jnp.bfloat16)
    held = lax.all_to_all(
        product.reshape(peers, chans, parts, LANES), ("tok", "span"), 0, 0, tiled=True
    )
    held = held.reshape(toks, spans, chans, parts, LANES).transpose(2, 3, 1, 0, 4)
    held = held.reshape(chans, parts, peers, LANES)
    first = lax.axis_index("span") * chans
    taps = lax.dynamic_slice_in_dim(long_filter, first, chans, 0)
    taps = taps.reshape(chans, blocks, LANES).astype(jnp.float32)
    gains = lax.dynamic_slice_in_dim(skip_gain, first, chans, 0)
    convolved = pl.pallas_call(
        functools.partial(conv_kernel, parts, peers, reach, blocks),
        grid=(chans,),
        in_specs=[
            pl.BlockSpec(memory_space=pltpu.SMEM),
            pl.BlockSpec((1, parts, peers, LANES), lambda c: (c, 0, 0, 0)),
            pl.BlockSpec((1, blocks, LANES), lambda c: (c, 0, 0)),
        ],
        out_specs=pl.BlockSpec((1, parts, peers, LANES), lambda c: (c, 0, 0, 0)),
        out_shape=jax.ShapeDtypeStruct((chans, parts, peers, LANES), jnp.bfloat16),
        scratch_shapes=[
            pltpu.VMEM((parts, reach + peers, LANES), jnp.float32),
            pltpu.VMEM(((blocks + 1) * LANES, LANES), jnp.bfloat16),
        ],
        compiler_params=pltpu.CompilerParams(vmem_limit_bytes=32 * 1024 * 1024),
    )(gains, held, taps)
    convolved = convolved.reshape(chans, parts, spans, toks, LANES).transpose(3, 2, 0, 1, 4)
    returned = lax.all_to_all(
        convolved.reshape(peers, chans, parts, LANES), ("tok", "span"), 0, 0, tiled=True
    )
    returned = lax.optimization_barrier(returned.reshape(D, tok_rows)).astype(jnp.float32)
    gated_rows = (query_rows * returned).astype(jnp.bfloat16)
    return lax.dot_general(
        gated_rows, w_out, (((0,), (0,)), ((), ())), preferred_element_type=jnp.float32
    ).astype(jnp.bfloat16)


def solution(mesh):
    return jax.shard_map(
        per_device,
        mesh=mesh,
        in_specs=(P(("span", "tok"), None), P(), P(), P("tok", None), P("tok"), P()),
        out_specs=P(("span", "tok"), None),
        check_vma=False,
    )
```

```python
import functools

import jax
import jax.numpy as jnp
from jax import lax
from jax.experimental import pallas as pl
from jax.experimental.pallas import tpu as pltpu
from jax.sharding import PartitionSpec as P

D = 256
LANES = 128
GROUP = 8
BAND = 16


def build_toeplitz(row_of, blocks, toeplitz_ref):
    row_at = lax.broadcasted_iota(jnp.int32, (LANES, LANES), 0)
    col_at = lax.broadcasted_iota(jnp.int32, (LANES, LANES), 1)
    upper = (col_at - row_at).astype(jnp.int16) >= 0

    def step(b, before):
        spread = jnp.broadcast_to(row_of(b), (BAND, LANES))
        band = pltpu.roll(spread, 0, 1, stride=1, stride_axis=0).astype(jnp.bfloat16)
        turned = jnp.concatenate(
            [band] + [pltpu.roll(band, i, 1) for i in range(BAND, LANES, BAND)], axis=0
        )
        toeplitz_ref[pl.ds(pl.multiple_of(b * LANES, LANES), LANES), :] = jnp.where(
            upper, turned, before
        )
        return turned

    nothing = jnp.zeros((LANES, LANES), jnp.bfloat16)
    last = lax.fori_loop(0, blocks, step, nothing, unroll=8)
    toeplitz_ref[blocks * LANES :, :] = jnp.where(upper, nothing, last)


def lagged(padded_ref, parts, rows, reach, lags):
    columns = []
    for b in lags:
        pieces = []
        for m in range(parts):
            back, part = divmod(m - b, parts)
            pieces.append(padded_ref[part, pl.ds(reach + back, rows), :])
        columns.append(jnp.concatenate(pieces, axis=0).astype(jnp.bfloat16))
    return jnp.concatenate(columns, axis=1) if len(columns) > 1 else columns[0]


def conv_channel(padded_ref, toeplitz_ref, parts, rows, reach, blocks):
    total = jnp.zeros((parts * rows, LANES), jnp.float32)
    for start in range(0, blocks + 1, GROUP):
        lags = range(start, min(start + GROUP, blocks + 1))
        total = total + jnp.dot(
            lagged(padded_ref, parts, rows, reach, lags),
            toeplitz_ref[start * LANES : (lags[-1] + 1) * LANES, :],
            preferred_element_type=jnp.float32,
        )
    return total


def conv_kernel(parts, rows, reach, blocks, gain_ref, x_ref, h_ref, y_ref, padded_ref, toeplitz_ref):
    build_toeplitz(lambda b: h_ref[0, pl.ds(b, 1), :], blocks, toeplitz_ref)
    padded_ref[:, :reach, :] = jnp.zeros((parts, reach, LANES), jnp.float32)
    padded_ref[:, reach:, :] = x_ref[0].astype(jnp.float32)
    total = conv_channel(padded_ref, toeplitz_ref, parts, rows, reach, blocks)
    gain = gain_ref[pl.program_id(0)]
    for m in range(parts):
        y_ref[0, m] = (total[m * rows : (m + 1) * rows] + gain * padded_ref[m, reach:, :]).astype(
            jnp.bfloat16
        )


def per_device(tokens, w_in, short_filter, long_filter, skip_gain, w_out):
    tok_rows = tokens.shape[0]
    spans, toks = lax.axis_size("span"), lax.axis_size("tok")
    peers = spans * toks
    parts = tok_rows // LANES
    taps_count = long_filter.shape[1]
    blocks = taps_count // LANES
    reach = -(-taps_count // tok_rows)
    chans = long_filter.shape[0] // spans
    pairs = [(i, i + 1) for i in range(peers - 1)]
    rim = lax.ppermute(tokens[tok_rows - 2 :], ("span", "tok"), pairs)
    projected = lax.dot_general(
        w_in,
        jnp.concatenate([rim, tokens], axis=0),
        (((0,), (1,)), ((), ())),
        preferred_element_type=jnp.float32,
    ).astype(jnp.bfloat16)
    padded = lax.optimization_barrier(projected).astype(jnp.float32)
    mixed = (
        short_filter[0][:, None] * padded[:, 2:]
        + short_filter[1][:, None] * padded[:, 1:-1]
        + short_filter[2][:, None] * padded[:, :-2]
    )
    query_rows = mixed[:D]
    product = (mixed[D : 2 * D] * mixed[2 * D :]).astype(jnp.bfloat16)
    held = lax.all_to_all(
        product.reshape(peers, chans, parts, LANES), ("tok", "span"), 0, 0, tiled=True
    )
    held = held.reshape(toks, spans, chans, parts, LANES).transpose(2, 3, 1, 0, 4)
    held = held.reshape(chans, parts, peers, LANES)
    first = lax.axis_index("span") * chans
    taps = lax.dynamic_slice_in_dim(long_filter, first, chans, 0)
    taps = taps.reshape(chans, blocks, LANES).astype(jnp.float32)
    gains = lax.dynamic_slice_in_dim(skip_gain, first, chans, 0)
    convolved = pl.pallas_call(
        functools.partial(conv_kernel, parts, peers, reach, blocks),
        grid=(chans,),
        in_specs=[
            pl.BlockSpec(memory_space=pltpu.SMEM),
            pl.BlockSpec((1, parts, peers, LANES), lambda c: (c, 0, 0, 0)),
            pl.BlockSpec((1, blocks, LANES), lambda c: (c, 0, 0)),
        ],
        out_specs=pl.BlockSpec((1, parts, peers, LANES), lambda c: (c, 0, 0, 0)),
        out_shape=jax.ShapeDtypeStruct((chans, parts, peers, LANES), jnp.bfloat16),
        scratch_shapes=[
            pltpu.VMEM((parts, reach + peers, LANES), jnp.float32),
            pltpu.VMEM(((blocks + 1) * LANES, LANES), jnp.bfloat16),
        ],
        compiler_params=pltpu.CompilerParams(vmem_limit_bytes=32 * 1024 * 1024),
    )(gains, held, taps)
    convolved = convolved.reshape(chans, parts, spans, toks, LANES).transpose(3, 2, 0, 1, 4)
    returned = lax.all_to_all(
        convolved.reshape(peers, chans, parts, LANES), ("tok", "span"), 0, 0, tiled=True
    )
    returned = lax.optimization_barrier(returned.reshape(D, tok_rows)).astype(jnp.float32)
    gated_rows = (query_rows * returned).astype(jnp.bfloat16)
    return lax.dot_general(
        gated_rows, w_out, (((0,), (0,)), ((), ())), preferred_element_type=jnp.float32
    ).astype(jnp.bfloat16)


def solution(mesh):
    return jax.shard_map(
        per_device,
        mesh=mesh,
        in_specs=(P(("span", "tok"), None), P(), P(), P("tok", None), P("tok"), P()),
        out_specs=P(("span", "tok"), None),
        check_vma=False,
    )
```

```python
import functools

import jax
import jax.numpy as jnp
from jax import lax
from jax.experimental import pallas as pl
from jax.experimental.pallas import tpu as pltpu
from jax.sharding import PartitionSpec as P

D = 256
LANES = 128
GROUP = 8
BAND = 16
RIM = 16
MESH = pl.DeviceIdType.MESH


def build_toeplitz(row_of, blocks, toeplitz_ref):
    row_at = lax.broadcasted_iota(jnp.int32, (LANES, LANES), 0)
    col_at = lax.broadcasted_iota(jnp.int32, (LANES, LANES), 1)
    upper = (col_at - row_at).astype(jnp.int16) >= 0

    def step(b, before):
        spread = jnp.broadcast_to(row_of(b), (BAND, LANES))
        band = pltpu.roll(spread, 0, 1, stride=1, stride_axis=0).astype(jnp.bfloat16)
        turned = jnp.concatenate(
            [band] + [pltpu.roll(band, i, 1) for i in range(BAND, LANES, BAND)], axis=0
        )
        toeplitz_ref[pl.ds(pl.multiple_of(b * LANES, LANES), LANES), :] = jnp.where(
            upper, turned, before
        )
        return turned

    nothing = jnp.zeros((LANES, LANES), jnp.bfloat16)
    last = lax.fori_loop(0, blocks, step, nothing, unroll=8)
    toeplitz_ref[blocks * LANES :, :] = jnp.where(upper, nothing, last)


def lagged(padded_ref, parts, rows, reach, lags):
    columns = []
    for b in lags:
        pieces = []
        for m in range(parts):
            back, part = divmod(m - b, parts)
            pieces.append(padded_ref[part, pl.ds(reach + back, rows), :])
        columns.append(jnp.concatenate(pieces, axis=0).astype(jnp.bfloat16))
    return jnp.concatenate(columns, axis=1) if len(columns) > 1 else columns[0]


def conv_channel(padded_ref, toeplitz_ref, parts, rows, reach, blocks):
    total = jnp.zeros((parts * rows, LANES), jnp.float32)
    for start in range(0, blocks + 1, GROUP):
        lags = range(start, min(start + GROUP, blocks + 1))
        total = total + jnp.dot(
            lagged(padded_ref, parts, rows, reach, lags),
            toeplitz_ref[start * LANES : (lags[-1] + 1) * LANES, :],
            preferred_element_type=jnp.float32,
        )
    return total


def whole_kernel(
    spans, toks, chans, parts, reach, blocks,
    gain_ref, tokens_ref, w_in_ref, short_ref, taps_ref, w_out_ref, out_ref,
    projected_ref, rim_ref, query_ref, sent_ref, held_ref, flat_ref, padded_ref,
    toeplitz_ref, result_ref, back_ref, returned_ref,
    rim_send, rim_recv, out_send, out_recv, back_send, back_recv,
):
    peers = spans * toks
    tok_rows = parts * LANES
    span_at, tok_at = lax.axis_index("span"), lax.axis_index("tok")
    me = span_at * toks + tok_at
    my_group = tok_at * spans + span_at

    def place(turn):
        return lax.div(turn, toks), lax.rem(turn, toks)

    def group_of(turn):
        return lax.rem(turn, toks) * spans + lax.div(turn, toks)

    barrier = pltpu.get_barrier_semaphore()

    def greet(i, carry):
        pl.semaphore_signal(
            barrier, inc=1, device_id=place(lax.rem(me + i, peers)), device_id_type=MESH
        )
        return carry

    lax.fori_loop(1, peers, greet, 0)

    def project(rows):
        return jnp.dot(rows, w_in_ref[...], preferred_element_type=jnp.float32).astype(
            jnp.bfloat16
        ).astype(jnp.float32)

    for m in range(parts):
        projected_ref[RIM + m * LANES : RIM + (m + 1) * LANES, :] = project(
            tokens_ref[m * LANES : (m + 1) * LANES, :]
        )
    pl.semaphore_wait(barrier, peers - 1)

    rim_copy = pltpu.make_async_remote_copy(
        src_ref=tokens_ref.at[pl.ds(tok_rows - RIM, RIM)],
        dst_ref=rim_ref,
        send_sem=rim_send,
        recv_sem=rim_recv,
        device_id=place(lax.rem(me + 1, peers)),
        device_id_type=MESH,
    )
    rim_copy.start()
    rim_copy.wait()
    projected_ref[:RIM, :] = jnp.where(me > 0, project(rim_ref[...]), 0.0)

    def mix(m, part):
        columns = slice(part * D, (part + 1) * D)
        first = RIM + m * LANES
        return (
            short_ref[0:1, columns] * projected_ref[first : first + LANES, columns]
            + short_ref[1:2, columns] * projected_ref[first - 1 : first - 1 + LANES, columns]
            + short_ref[2:3, columns] * projected_ref[first - 2 : first - 2 + LANES, columns]
        )

    turned = []
    for m in range(parts):
        product = mix(m, 1) * mix(m, 2)
        turned.append(product.T.reshape(peers, chans, LANES))
    sent_ref[...] = jnp.concatenate(turned, axis=1).astype(jnp.bfloat16)

    def out_copy(turn):
        return pltpu.make_async_remote_copy(
            src_ref=sent_ref.at[group_of(turn)],
            dst_ref=held_ref.at[me],
            send_sem=out_send.at[turn],
            recv_sem=out_recv.at[me],
            device_id=place(turn),
            device_id_type=MESH,
        )

    def out_arrival(turn):
        return pltpu.make_async_remote_copy(
            src_ref=sent_ref.at[my_group],
            dst_ref=held_ref.at[turn],
            send_sem=out_send.at[turn],
            recv_sem=out_recv.at[turn],
            device_id=place(turn),
            device_id_type=MESH,
        )

    def back_copy(turn):
        return pltpu.make_async_remote_copy(
            src_ref=back_ref.at[turn],
            dst_ref=returned_ref.at[my_group],
            send_sem=back_send.at[turn],
            recv_sem=back_recv.at[me],
            device_id=place(turn),
            device_id_type=MESH,
        )

    def back_arrival(turn):
        return pltpu.make_async_remote_copy(
            src_ref=back_ref.at[me],
            dst_ref=returned_ref.at[group_of(turn)],
            send_sem=back_send.at[turn],
            recv_sem=back_recv.at[turn],
            device_id=place(turn),
            device_id_type=MESH,
        )

    def each_peer(act):
        def step(i, carry):
            act(lax.rem(me + i, peers))
            return carry

        lax.fori_loop(1, peers, step, 0)

    each_peer(lambda turn: out_copy(turn).start())
    held_ref[me] = sent_ref[my_group]

    def build(c, carry):
        build_toeplitz(
            lambda b: taps_ref[c, pl.ds(b, 1), :],
            blocks,
            toeplitz_ref.at[c],
        )
        return carry

    lax.fori_loop(0, chans, build, 0)
    for m in range(parts):
        query_ref[m * LANES : (m + 1) * LANES, :] = mix(m, 0)
    padded_ref[:, :reach, :] = jnp.zeros((parts, reach, LANES), jnp.float32)

    each_peer(lambda turn: out_arrival(turn).wait_recv())
    flat_ref[...] = held_ref[...].astype(jnp.float32).reshape(peers * parts * chans, LANES)

    def convolve(c, carry):
        for m in range(parts):
            padded_ref[m, reach:, :] = flat_ref[pl.ds(m * chans + c, peers, stride=parts * chans), :]
        total = conv_channel(padded_ref, toeplitz_ref.at[c], parts, peers, reach, blocks)
        gain = gain_ref[c]
        for m in range(parts):
            result_ref[pl.ds(m * chans + c, peers, stride=parts * chans), :] = (
                total[m * peers : (m + 1) * peers] + gain * padded_ref[m, reach:, :]
            )
        return carry

    lax.fori_loop(0, chans, convolve, 0)
    back_ref[...] = result_ref[...].reshape(peers, parts * chans, LANES).astype(jnp.bfloat16)
    each_peer(lambda turn: back_copy(turn).start())
    returned_ref[my_group] = back_ref[me]
    each_peer(lambda turn: back_arrival(turn).wait_recv())
    returned = returned_ref[...].astype(jnp.float32)
    for m in range(parts):
        convolved = returned[:, m * chans : (m + 1) * chans, :].reshape(D, LANES).T
        gated = (query_ref[m * LANES : (m + 1) * LANES, :] * convolved).astype(jnp.bfloat16)
        out_ref[m * LANES : (m + 1) * LANES, :] = jnp.dot(
            gated, w_out_ref[...], preferred_element_type=jnp.float32
        ).astype(jnp.bfloat16)
    each_peer(lambda turn: out_copy(turn).wait_send())
    each_peer(lambda turn: back_copy(turn).wait_send())


def per_device(tokens, w_in, short_filter, long_filter, skip_gain, w_out):
    tok_rows = tokens.shape[0]
    spans, toks = lax.axis_size("span"), lax.axis_size("tok")
    peers = spans * toks
    parts = tok_rows // LANES
    taps_count = long_filter.shape[1]
    blocks = taps_count // LANES
    reach = -(-taps_count // tok_rows)
    chans = long_filter.shape[0] // spans
    first = lax.axis_index("span") * chans
    taps = lax.dynamic_slice_in_dim(long_filter, first, chans, 0)
    taps = taps.reshape(chans, blocks, LANES).astype(jnp.float32)
    gains = lax.dynamic_slice_in_dim(skip_gain, first, chans, 0)
    vmem = pl.BlockSpec(memory_space=pltpu.VMEM)
    piece = (peers, parts * chans, LANES)
    flat = (peers * parts * chans, LANES)
    return pl.pallas_call(
        functools.partial(whole_kernel, spans, toks, chans, parts, reach, blocks),
        in_specs=[pl.BlockSpec(memory_space=pltpu.SMEM)] + [vmem] * 5,
        out_specs=vmem,
        out_shape=jax.ShapeDtypeStruct((tok_rows, D), jnp.bfloat16),
        scratch_shapes=[
            pltpu.VMEM((RIM + tok_rows, 3 * D), jnp.float32),
            pltpu.VMEM((RIM, D), jnp.bfloat16),
            pltpu.VMEM((tok_rows, D), jnp.float32),
            pltpu.VMEM(piece, jnp.bfloat16),
            pltpu.VMEM(piece, jnp.bfloat16),
            pltpu.VMEM(flat, jnp.float32),
            pltpu.VMEM((parts, reach + peers, LANES), jnp.float32),
            pltpu.VMEM((chans, (blocks + 1) * LANES, LANES), jnp.bfloat16),
            pltpu.VMEM(flat, jnp.float32),
            pltpu.VMEM(piece, jnp.bfloat16),
            pltpu.VMEM(piece, jnp.bfloat16),
            pltpu.SemaphoreType.DMA,
            pltpu.SemaphoreType.DMA,
            pltpu.SemaphoreType.DMA((peers,)),
            pltpu.SemaphoreType.DMA((peers,)),
            pltpu.SemaphoreType.DMA((peers,)),
            pltpu.SemaphoreType.DMA((peers,)),
        ],
        compiler_params=pltpu.CompilerParams(
            collective_id=0, has_side_effects=True, vmem_limit_bytes=48 * 1024 * 1024
        ),
    )(gains, tokens, w_in, short_filter, taps, w_out)


def solution(mesh):
    return jax.shard_map(
        per_device,
        mesh=mesh,
        in_specs=(P(("span", "tok"), None), P(), P(), P("tok", None), P("tok"), P()),
        out_specs=P(("span", "tok"), None),
        check_vma=False,
    )
```

```python
import functools

import jax
import jax.numpy as jnp
from jax import lax
from jax.experimental import pallas as pl
from jax.experimental.pallas import tpu as pltpu
from jax.sharding import PartitionSpec as P

D = 256
LANES = 128
GROUP = 8
BAND = 16
RIM = 16
MESH = pl.DeviceIdType.MESH


def build_toeplitz(row_of, blocks, toeplitz_ref):
    row_at = lax.broadcasted_iota(jnp.int32, (LANES, LANES), 0)
    col_at = lax.broadcasted_iota(jnp.int32, (LANES, LANES), 1)
    upper = (col_at - row_at).astype(jnp.int16) >= 0

    def step(b, before):
        spread = jnp.broadcast_to(row_of(b), (BAND, LANES))
        band = pltpu.roll(spread, 0, 1, stride=1, stride_axis=0).astype(jnp.bfloat16)
        turned = jnp.concatenate(
            [band] + [pltpu.roll(band, i, 1) for i in range(BAND, LANES, BAND)], axis=0
        )
        toeplitz_ref[pl.ds(pl.multiple_of(b * LANES, LANES), LANES), :] = jnp.where(
            upper, turned, before
        )
        return turned

    nothing = jnp.zeros((LANES, LANES), jnp.bfloat16)
    last = lax.fori_loop(0, blocks, step, nothing, unroll=8)
    toeplitz_ref[blocks * LANES :, :] = jnp.where(upper, nothing, last)


def lagged(padded_ref, parts, rows, reach, lags):
    seen = {}

    def piece(lag, m):
        back, part = divmod(m - lag, parts)
        if (back, part) not in seen:
            rows_at = padded_ref[part, pl.ds(reach + back, rows), :]
            seen[back, part] = rows_at.astype(jnp.bfloat16)
        return seen[back, part]

    columns = [jnp.concatenate([piece(b, m) for m in range(parts)], axis=0) for b in lags]
    return jnp.concatenate(columns, axis=1) if len(columns) > 1 else columns[0]


def conv_channel(padded_ref, toeplitz_ref, parts, rows, reach, blocks):
    total = jnp.zeros((parts * rows, LANES), jnp.float32)
    for start in range(0, blocks + 1, GROUP):
        lags = range(start, min(start + GROUP, blocks + 1))
        total = total + jnp.dot(
            lagged(padded_ref, parts, rows, reach, lags),
            toeplitz_ref[start * LANES : (lags[-1] + 1) * LANES, :],
            preferred_element_type=jnp.float32,
        )
    return total


def halves_of(chans):
    return 2 if chans % 8 == 0 else 1


def exchanged(first, second, half):
    low = lax.broadcasted_iota(jnp.int32, first.shape, 1) < half
    return (
        jnp.where(low, first, pltpu.roll(second, half, 1)),
        jnp.where(low, pltpu.roll(first, half, 1), second),
    )


def whole_kernel(
    spans, toks, chans, parts, reach, blocks,
    gain_ref, tokens_hbm, w_in_hbm, short_hbm, filter_hbm, w_out_hbm, out_ref,
    tokens_ref, w_in_ref, short_ref, filter_ref, w_out_ref, taps_ref,
    projected_ref, rim_ref, sent_ref, held_ref, flat_ref, padded_ref,
    toeplitz_ref, result_ref, back_ref, returned_ref,
    load_sem, rim_send, rim_recv, out_send, out_recv, back_send, back_recv,
):
    peers = spans * toks
    tok_rows = parts * LANES
    halves = halves_of(chans)
    group = chans // halves
    rows = parts * group
    span_at, tok_at = lax.axis_index("span"), lax.axis_index("tok")
    me = span_at * toks + tok_at
    my_group = tok_at * spans + span_at
    first_chan = span_at * chans
    chan_offset = lax.rem(first_chan, RIM)

    def place(turn):
        return lax.div(turn, toks), lax.rem(turn, toks)

    def group_of(turn):
        return lax.rem(turn, toks) * spans + lax.div(turn, toks)

    def each_peer(act):
        def step(i, carry):
            act(lax.rem(me + i, peers))
            return carry

        lax.fori_loop(1, peers, step, 0)

    loads = [
        pltpu.make_async_copy(source, target, load_sem.at[i])
        for i, (source, target) in enumerate(
            [
                (tokens_hbm, tokens_ref),
                (w_in_hbm, w_in_ref),
                (
                    filter_hbm.at[pl.ds(pl.multiple_of(first_chan - chan_offset, RIM), RIM)],
                    filter_ref,
                ),
                (short_hbm, short_ref),
                (w_out_hbm, w_out_ref),
            ]
        )
    ]
    for load in loads:
        load.start()
    barrier = pltpu.get_barrier_semaphore()
    each_peer(
        lambda turn: pl.semaphore_signal(
            barrier, inc=1, device_id=place(turn), device_id_type=MESH
        )
    )

    def project(values):
        return jnp.dot(values, w_in_ref[...], preferred_element_type=jnp.float32).astype(
            jnp.bfloat16
        ).astype(jnp.float32)

    loads[0].wait()
    loads[1].wait()
    for m in range(parts):
        projected_ref[RIM + m * LANES : RIM + (m + 1) * LANES, :] = project(
            tokens_ref[m * LANES : (m + 1) * LANES, :]
        )
    loads[2].wait()
    for b in range(blocks):
        taps_ref[b] = filter_ref[:, b * LANES : (b + 1) * LANES].astype(jnp.float32)
    loads[3].wait()
    loads[4].wait()
    pl.semaphore_wait(barrier, peers - 1)

    rim_copy = pltpu.make_async_remote_copy(
        src_ref=tokens_ref.at[pl.ds(tok_rows - RIM, RIM)],
        dst_ref=rim_ref,
        send_sem=rim_send,
        recv_sem=rim_recv,
        device_id=place(lax.rem(me + 1, peers)),
        device_id_type=MESH,
    )
    rim_copy.start()

    def build(c, carry):
        build_toeplitz(
            lambda b: taps_ref[b, pl.ds(chan_offset + c, 1), :], blocks, toeplitz_ref.at[c]
        )
        return carry

    lax.fori_loop(0, 1, build, 0)
    rim_copy.wait()
    projected_ref[:RIM, :] = jnp.where(me > 0, project(rim_ref[...]), 0.0)

    def mix(m, part):
        columns = slice(part * D, (part + 1) * D)
        first = RIM + m * LANES
        return (
            short_ref[0:1, columns] * projected_ref[first : first + LANES, columns]
            + short_ref[1:2, columns] * projected_ref[first - 1 : first - 1 + LANES, columns]
            + short_ref[2:3, columns] * projected_ref[first - 2 : first - 2 + LANES, columns]
        )

    turned = [
        (mix(m, 1) * mix(m, 2)).T.reshape(peers, chans, LANES) for m in range(parts)
    ]
    if halves == 1:
        sent_ref[0] = jnp.concatenate(turned, axis=1).astype(jnp.bfloat16)
    else:
        mated = [exchanged(turned[m], turned[m + 1], group) for m in range(0, parts, 2)]
        for h in range(halves):
            sent_ref[h] = jnp.concatenate([pair[h] for pair in mated], axis=1).astype(
                jnp.bfloat16
            )

    def out_copy(h, turn):
        return pltpu.make_async_remote_copy(
            src_ref=sent_ref.at[h, group_of(turn)],
            dst_ref=held_ref.at[h, me],
            send_sem=out_send.at[h],
            recv_sem=out_recv.at[h],
            device_id=place(turn),
            device_id_type=MESH,
        )

    def back_copy(h, turn):
        return pltpu.make_async_remote_copy(
            src_ref=back_ref.at[h, turn],
            dst_ref=returned_ref.at[h, my_group],
            send_sem=back_send.at[h],
            recv_sem=back_recv.at[h],
            device_id=place(turn),
            device_id_type=MESH,
        )

    def all_of(h, source, target, send_sem, recv_sem):
        return pltpu.make_async_remote_copy(
            src_ref=source.at[h, pl.ds(0, peers - 1)],
            dst_ref=target.at[h, pl.ds(0, peers - 1)],
            send_sem=send_sem.at[h],
            recv_sem=recv_sem.at[h],
            device_id=place(lax.rem(me + 1, peers)),
            device_id_type=MESH,
        )

    for h in range(halves):
        each_peer(lambda turn: out_copy(h, turn).start())
        held_ref[h, me] = sent_ref[h, my_group]
    padded_ref[:, :reach, :] = jnp.zeros((parts, reach, LANES), jnp.float32)

    for h in range(halves):
        lax.fori_loop(max(1, h * group), (h + 1) * group, build, 0)
        all_of(h, sent_ref, held_ref, out_send, out_recv).wait_recv()
        flat_ref[...] = held_ref[h].astype(jnp.float32).reshape(peers * rows, LANES)

        def convolve(c, carry):
            for m in range(parts):
                padded_ref[m, reach:, :] = flat_ref[pl.ds(m * group + c, peers, stride=rows), :]
            at = h * group + c
            total = conv_channel(padded_ref, toeplitz_ref.at[at], parts, peers, reach, blocks)
            gain = gain_ref[first_chan + at]
            for m in range(parts):
                result_ref[pl.ds(m * group + c, peers, stride=rows), :] = (
                    total[m * peers : (m + 1) * peers] + gain * padded_ref[m, reach:, :]
                )
            return carry

        lax.fori_loop(0, group, convolve, 0)
        back_ref[h] = result_ref[...].reshape(peers, rows, LANES).astype(jnp.bfloat16)
        each_peer(lambda turn: back_copy(h, turn).start())
        returned_ref[h, my_group] = back_ref[h, me]

    query = [mix(m, 0) for m in range(parts)]
    for h in range(halves):
        all_of(h, back_ref, returned_ref, back_send, back_recv).wait_recv()
    if halves == 1:
        whole = returned_ref[0].astype(jnp.float32)
        pieces = [whole[:, m * chans : (m + 1) * chans, :] for m in range(parts)]
    else:
        pieces = []
        for m in range(0, parts, 2):
            pair = slice(m * group, (m + 2) * group)
            pieces += exchanged(
                *[returned_ref[h, :, pair, :].astype(jnp.float32) for h in range(halves)], group
            )
    for m in range(parts):
        gated = (query[m] * pieces[m].reshape(D, LANES).T).astype(jnp.bfloat16)
        out_ref[m * LANES : (m + 1) * LANES, :] = jnp.dot(
            gated, w_out_ref[...], preferred_element_type=jnp.float32
        ).astype(jnp.bfloat16)
    for h in range(halves):
        all_of(h, sent_ref, held_ref, out_send, out_recv).wait_send()
        all_of(h, back_ref, returned_ref, back_send, back_recv).wait_send()


def per_device(tokens, w_in, short_filter, long_filter, skip_gain, w_out):
    tok_rows = tokens.shape[0]
    spans, toks = lax.axis_size("span"), lax.axis_size("tok")
    peers = spans * toks
    parts = tok_rows // LANES
    taps_count = long_filter.shape[1]
    blocks = taps_count // LANES
    reach = -(-taps_count // tok_rows)
    chans = long_filter.shape[0] // spans
    halves = halves_of(chans)
    rows = parts * chans // halves
    piece = (halves, peers, rows, LANES)
    flat = (peers * rows, LANES)
    return pl.pallas_call(
        functools.partial(whole_kernel, spans, toks, chans, parts, reach, blocks),
        in_specs=[pl.BlockSpec(memory_space=pltpu.SMEM)]
        + [pl.BlockSpec(memory_space=pl.ANY)] * 5,
        out_specs=pl.BlockSpec(memory_space=pltpu.VMEM),
        out_shape=jax.ShapeDtypeStruct((tok_rows, D), jnp.bfloat16),
        scratch_shapes=[
            pltpu.VMEM(tokens.shape, tokens.dtype),
            pltpu.VMEM(w_in.shape, w_in.dtype),
            pltpu.VMEM(short_filter.shape, short_filter.dtype),
            pltpu.VMEM((RIM, taps_count), long_filter.dtype),
            pltpu.VMEM(w_out.shape, w_out.dtype),
            pltpu.VMEM((blocks, RIM, LANES), jnp.float32),
            pltpu.VMEM((RIM + tok_rows, 3 * D), jnp.float32),
            pltpu.VMEM((RIM, D), jnp.bfloat16),
            pltpu.VMEM(piece, jnp.bfloat16),
            pltpu.VMEM(piece, jnp.bfloat16),
            pltpu.VMEM(flat, jnp.float32),
            pltpu.VMEM((parts, reach + peers, LANES), jnp.float32),
            pltpu.VMEM((chans, (blocks + 1) * LANES, LANES), jnp.bfloat16),
            pltpu.VMEM(flat, jnp.float32),
            pltpu.VMEM(piece, jnp.bfloat16),
            pltpu.VMEM(piece, jnp.bfloat16),
            pltpu.SemaphoreType.DMA((5,)),
            pltpu.SemaphoreType.DMA,
            pltpu.SemaphoreType.DMA,
            pltpu.SemaphoreType.DMA((halves,)),
            pltpu.SemaphoreType.DMA((halves,)),
            pltpu.SemaphoreType.DMA((halves,)),
            pltpu.SemaphoreType.DMA((halves,)),
        ],
        compiler_params=pltpu.CompilerParams(
            collective_id=0, has_side_effects=True, vmem_limit_bytes=48 * 1024 * 1024
        ),
    )(skip_gain, tokens, w_in, short_filter, long_filter, w_out)


def solution(mesh):
    return jax.shard_map(
        per_device,
        mesh=mesh,
        in_specs=(P(("span", "tok"), None), P(), P(), P("tok", None), P("tok"), P()),
        out_specs=P(("span", "tok"), None),
        check_vma=False,
    )
```

```python
import functools

import jax
import jax.numpy as jnp
from jax import lax
from jax.experimental import pallas as pl
from jax.experimental.pallas import tpu as pltpu
from jax.sharding import PartitionSpec as P

D = 256
LANES = 128
GROUP = 8
BAND = 16
RIM = 16
MESH = pl.DeviceIdType.MESH


def upper_mask():
    row_at = lax.broadcasted_iota(jnp.int32, (LANES, LANES), 0)
    col_at = lax.broadcasted_iota(jnp.int32, (LANES, LANES), 1)
    return (col_at - row_at).astype(jnp.int16) >= 0


def toeplitz_block(row, before, upper):
    spread = jnp.broadcast_to(row, (BAND, LANES))
    band = pltpu.roll(spread, 0, 1, stride=1, stride_axis=0).astype(jnp.bfloat16)
    turned = jnp.concatenate(
        [band] + [pltpu.roll(band, i, 1) for i in range(BAND, LANES, BAND)], axis=0
    )
    return turned, jnp.where(upper, turned, before)


def build_toeplitz(row_of, blocks, toeplitz_ref):
    upper = upper_mask()

    def step(b, before):
        turned, block = toeplitz_block(row_of(b), before, upper)
        toeplitz_ref[pl.ds(pl.multiple_of(b * LANES, LANES), LANES), :] = block
        return turned

    nothing = jnp.zeros((LANES, LANES), jnp.bfloat16)
    last = lax.fori_loop(0, blocks, step, nothing, unroll=8)
    toeplitz_ref[blocks * LANES :, :] = jnp.where(upper, nothing, last)


def lagged(padded_ref, parts, rows, reach, lags):
    seen = {}

    def piece(lag, m):
        back, part = divmod(m - lag, parts)
        if (back, part) not in seen:
            rows_at = padded_ref[part, pl.ds(reach + back, rows), :]
            seen[back, part] = rows_at.astype(jnp.bfloat16)
        return seen[back, part]

    columns = [jnp.concatenate([piece(b, m) for m in range(parts)], axis=0) for b in lags]
    return jnp.concatenate(columns, axis=1) if len(columns) > 1 else columns[0]


def conv_channel(padded_ref, toeplitz_ref, parts, rows, reach, blocks, row_of=None, next_ref=None):
    total = jnp.zeros((parts * rows, LANES), jnp.float32)
    if next_ref is not None:
        upper = upper_mask()
        nothing = before = jnp.zeros((LANES, LANES), jnp.bfloat16)
    for start in range(0, blocks + 1, GROUP):
        lags = range(start, min(start + GROUP, blocks + 1))
        total = total + jnp.dot(
            lagged(padded_ref, parts, rows, reach, lags),
            toeplitz_ref[start * LANES : (lags[-1] + 1) * LANES, :],
            preferred_element_type=jnp.float32,
        )
        if next_ref is not None:
            for b in lags:
                if b < blocks:
                    before, block = toeplitz_block(row_of(b), before, upper)
                else:
                    block = jnp.where(upper, nothing, before)
                next_ref[b * LANES : (b + 1) * LANES, :] = block
    return total


def halves_of(chans):
    return 2 if chans % 8 == 0 else 1


def exchanged(first, second, half):
    low = lax.broadcasted_iota(jnp.int32, first.shape, 1) < half
    return (
        jnp.where(low, first, pltpu.roll(second, half, 1)),
        jnp.where(low, pltpu.roll(first, half, 1), second),
    )


def whole_kernel(
    spans, toks, chans, parts, reach, blocks,
    gain_hbm, tokens_hbm, w_in_hbm, short_hbm, filter_hbm, w_out_hbm, out_ref,
    gain_ref, tokens_ref, w_in_ref, short_ref, filter_ref, w_out_ref, taps_ref,
    projected_ref, rim_ref, sent_ref, held_ref, flat_ref, padded_ref,
    toeplitz_refs, result_ref, back_ref, returned_ref,
    load_sem, rim_send, rim_recv, out_send, out_recv, back_send, back_recv,
):
    peers = spans * toks
    tok_rows = parts * LANES
    halves = halves_of(chans)
    group = chans // halves
    rows = parts * group
    span_at, tok_at = lax.axis_index("span"), lax.axis_index("tok")
    me = span_at * toks + tok_at
    my_group = tok_at * spans + span_at
    first_chan = span_at * chans
    chan_offset = lax.rem(first_chan, RIM)

    def shifted(at, by, size):
        moved = at + by
        return jnp.where(moved >= size, moved - size, moved)

    def each_peer(act):
        for j in range(1, toks):
            act(span_at, shifted(tok_at, j, toks))

        def step(i, carry):
            for j in range(toks):
                act(shifted(span_at, i, spans), shifted(tok_at, j, toks))
            return carry

        lax.fori_loop(1, spans, step, 0)

    loads = [
        pltpu.make_async_copy(source, target, load_sem.at[i])
        for i, (source, target) in enumerate(
            [
                (tokens_hbm, tokens_ref),
                (w_in_hbm, w_in_ref),
                (
                    filter_hbm.at[pl.ds(pl.multiple_of(first_chan - chan_offset, RIM), RIM)],
                    filter_ref,
                ),
                (short_hbm, short_ref),
                (w_out_hbm, w_out_ref),
                (gain_hbm, gain_ref),
            ]
        )
    ]
    for load in loads:
        load.start()
    barrier = pltpu.get_barrier_semaphore()
    each_peer(
        lambda span, tok: pl.semaphore_signal(
            barrier, inc=1, device_id=(span, tok), device_id_type=MESH
        )
    )

    def project(values):
        return jnp.dot(values, w_in_ref[...], preferred_element_type=jnp.float32).astype(
            jnp.bfloat16
        ).astype(jnp.float32)

    loads[0].wait()
    loads[1].wait()
    for m in range(parts):
        projected_ref[RIM + m * LANES : RIM + (m + 1) * LANES, :] = project(
            tokens_ref[m * LANES : (m + 1) * LANES, :]
        )
    loads[2].wait()
    for b in range(blocks):
        taps_ref[b] = filter_ref[:, b * LANES : (b + 1) * LANES].astype(jnp.float32)
    loads[3].wait()
    loads[4].wait()
    loads[5].wait()
    pl.semaphore_wait(barrier, peers - 1)

    follower = lax.rem(me + 1, peers)
    following = (lax.div(follower, toks), lax.rem(follower, toks))
    rim_copy = pltpu.make_async_remote_copy(
        src_ref=tokens_ref.at[pl.ds(tok_rows - RIM, RIM)],
        dst_ref=rim_ref,
        send_sem=rim_send,
        recv_sem=rim_recv,
        device_id=following,
        device_id_type=MESH,
    )
    rim_copy.start()

    def mix(m, part):
        columns = slice(part * D, (part + 1) * D)
        first = RIM + m * LANES
        return (
            short_ref[0:1, columns] * projected_ref[first : first + LANES, columns]
            + short_ref[1:2, columns] * projected_ref[first - 1 : first - 1 + LANES, columns]
            + short_ref[2:3, columns] * projected_ref[first - 2 : first - 2 + LANES, columns]
        )

    def turned_product(m):
        return (mix(m, 1) * mix(m, 2)).T.reshape(peers, chans, LANES)

    turned = [turned_product(m) for m in range(1, parts)]
    rim_copy.wait()
    projected_ref[:RIM, :] = jnp.where(me > 0, project(rim_ref[...]), 0.0)
    turned = [turned_product(0)] + turned
    if halves == 1:
        sent_ref[0] = jnp.concatenate(turned, axis=1).astype(jnp.bfloat16)
    else:
        mated = [exchanged(turned[m], turned[m + 1], group) for m in range(0, parts, 2)]
        for h in range(halves):
            sent_ref[h] = jnp.concatenate([pair[h] for pair in mated], axis=1).astype(
                jnp.bfloat16
            )

    def out_copy(h, span, tok):
        return pltpu.make_async_remote_copy(
            src_ref=sent_ref.at[h, tok * spans + span],
            dst_ref=held_ref.at[h, me],
            send_sem=out_send.at[h],
            recv_sem=out_recv.at[h],
            device_id=(span, tok),
            device_id_type=MESH,
        )

    def back_copy(h, span, tok):
        return pltpu.make_async_remote_copy(
            src_ref=back_ref.at[h, span * toks + tok],
            dst_ref=returned_ref.at[h, my_group],
            send_sem=back_send.at[h],
            recv_sem=back_recv.at[h],
            device_id=(span, tok),
            device_id_type=MESH,
        )

    def all_of(h, source, target, send_sem, recv_sem):
        return pltpu.make_async_remote_copy(
            src_ref=source.at[h, pl.ds(0, peers - 1)],
            dst_ref=target.at[h, pl.ds(0, peers - 1)],
            send_sem=send_sem.at[h],
            recv_sem=recv_sem.at[h],
            device_id=following,
            device_id_type=MESH,
        )

    for h in range(halves):
        each_peer(lambda span, tok: out_copy(h, span, tok).start())
        held_ref[h, me] = sent_ref[h, my_group]

    def row_of(at):
        return lambda b: taps_ref[b, pl.ds(chan_offset + at, 1), :]

    def build(c, carry):
        build_toeplitz(row_of(c), blocks, toeplitz_refs[0].at[c])
        return carry

    padded_ref[:, :reach, :] = jnp.zeros((parts, reach, LANES), jnp.float32)

    for h in range(halves):
        if h == 0:
            lax.fori_loop(0, group, build, 0)
        all_of(h, sent_ref, held_ref, out_send, out_recv).wait_recv()
        flat_ref[...] = held_ref[h].astype(jnp.float32).reshape(peers * rows, LANES)

        def convolve(c, carry):
            for m in range(parts):
                padded_ref[m, reach:, :] = flat_ref[pl.ds(m * group + c, peers, stride=rows), :]
            at = h * group + c
            ahead = (row_of(at + group), toeplitz_refs[h + 1].at[c]) if h + 1 < halves else ()
            total = conv_channel(
                padded_ref, toeplitz_refs[h].at[c], parts, peers, reach, blocks, *ahead
            )
            gain = gain_ref[first_chan + at]
            for m in range(parts):
                result_ref[pl.ds(m * group + c, peers, stride=rows), :] = (
                    total[m * peers : (m + 1) * peers] + gain * padded_ref[m, reach:, :]
                )
            return carry

        lax.fori_loop(0, group, convolve, 0)
        back_ref[h] = result_ref[...].reshape(peers, rows, LANES).astype(jnp.bfloat16)
        each_peer(lambda span, tok: back_copy(h, span, tok).start())
        returned_ref[h, my_group] = back_ref[h, me]

    query = [mix(m, 0) for m in range(parts)]
    for h in range(halves):
        all_of(h, back_ref, returned_ref, back_send, back_recv).wait_recv()
    if halves == 1:
        whole = returned_ref[0].astype(jnp.float32)
        pieces = [whole[:, m * chans : (m + 1) * chans, :] for m in range(parts)]
    else:
        pieces = []
        for m in range(0, parts, 2):
            pair = slice(m * group, (m + 2) * group)
            pieces += exchanged(
                *[returned_ref[h, :, pair, :].astype(jnp.float32) for h in range(halves)], group
            )
    for m in range(parts):
        gated = (query[m] * pieces[m].reshape(D, LANES).T).astype(jnp.bfloat16)
        out_ref[m * LANES : (m + 1) * LANES, :] = jnp.dot(
            gated, w_out_ref[...], preferred_element_type=jnp.float32
        ).astype(jnp.bfloat16)
    for h in range(halves):
        all_of(h, sent_ref, held_ref, out_send, out_recv).wait_send()
        all_of(h, back_ref, returned_ref, back_send, back_recv).wait_send()


def per_device(tokens, w_in, short_filter, long_filter, skip_gain, w_out):
    tok_rows = tokens.shape[0]
    spans, toks = lax.axis_size("span"), lax.axis_size("tok")
    peers = spans * toks
    parts = tok_rows // LANES
    taps_count = long_filter.shape[1]
    blocks = taps_count // LANES
    reach = -(-taps_count // tok_rows)
    chans = long_filter.shape[0] // spans
    halves = halves_of(chans)
    rows = parts * chans // halves
    piece = (halves, peers, rows, LANES)
    flat = (peers * rows, LANES)
    return pl.pallas_call(
        functools.partial(whole_kernel, spans, toks, chans, parts, reach, blocks),
        in_specs=[pl.BlockSpec(memory_space=pltpu.HBM)] * 6,
        out_specs=pl.BlockSpec(memory_space=pltpu.VMEM),
        out_shape=jax.ShapeDtypeStruct((tok_rows, D), jnp.bfloat16),
        scratch_shapes=[
            pltpu.SMEM(skip_gain.shape, skip_gain.dtype),
            pltpu.VMEM(tokens.shape, tokens.dtype),
            pltpu.VMEM(w_in.shape, w_in.dtype),
            pltpu.VMEM(short_filter.shape, short_filter.dtype),
            pltpu.VMEM((RIM, taps_count), long_filter.dtype),
            pltpu.VMEM(w_out.shape, w_out.dtype),
            pltpu.VMEM((blocks, RIM, LANES), jnp.float32),
            pltpu.VMEM((RIM + tok_rows, 3 * D), jnp.float32),
            pltpu.VMEM((RIM, D), jnp.bfloat16),
            pltpu.VMEM(piece, jnp.bfloat16),
            pltpu.VMEM(piece, jnp.bfloat16),
            pltpu.VMEM(flat, jnp.float32),
            pltpu.VMEM((parts, reach + peers, LANES), jnp.float32),
            [pltpu.VMEM((chans // halves, (blocks + 1) * LANES, LANES), jnp.bfloat16)] * halves,
            pltpu.VMEM(flat, jnp.float32),
            pltpu.VMEM(piece, jnp.bfloat16),
            pltpu.VMEM(piece, jnp.bfloat16),
            pltpu.SemaphoreType.DMA((6,)),
            pltpu.SemaphoreType.DMA,
            pltpu.SemaphoreType.DMA,
            pltpu.SemaphoreType.DMA((halves,)),
            pltpu.SemaphoreType.DMA((halves,)),
            pltpu.SemaphoreType.DMA((halves,)),
            pltpu.SemaphoreType.DMA((halves,)),
        ],
        compiler_params=pltpu.CompilerParams(
            collective_id=0, has_side_effects=True, vmem_limit_bytes=60 * 1024 * 1024
        ),
    )(skip_gain, tokens, w_in, short_filter, long_filter, w_out)


def solution(mesh):
    return jax.shard_map(
        per_device,
        mesh=mesh,
        in_specs=(P(("span", "tok"), None), P(), P(), P("tok", None), P("tok"), P()),
        out_specs=P(("span", "tok"), None),
        check_vma=False,
    )
```

```python
import functools

import jax
import jax.numpy as jnp
from jax import lax
from jax.experimental import pallas as pl
from jax.experimental.pallas import tpu as pltpu
from jax.sharding import PartitionSpec as P

D = 256
LANES = 128
GROUP = 8
BAND = 16
RIM = 16
MESH = pl.DeviceIdType.MESH


def upper_mask():
    row_at = lax.broadcasted_iota(jnp.int32, (LANES, LANES), 0)
    col_at = lax.broadcasted_iota(jnp.int32, (LANES, LANES), 1)
    return (col_at - row_at).astype(jnp.int16) >= 0


def toeplitz_block(row, before, upper):
    spread = jnp.broadcast_to(row, (BAND, LANES))
    band = pltpu.roll(spread, 0, 1, stride=1, stride_axis=0).astype(jnp.bfloat16)
    turned = jnp.concatenate(
        [band] + [pltpu.roll(band, i, 1) for i in range(BAND, LANES, BAND)], axis=0
    )
    return turned, jnp.where(upper, turned, before)


def build_toeplitz(row_of, blocks, toeplitz_ref):
    upper = upper_mask()

    def step(b, before):
        turned, block = toeplitz_block(row_of(b), before, upper)
        toeplitz_ref[pl.ds(pl.multiple_of(b * LANES, LANES), LANES), :] = block
        return turned

    nothing = jnp.zeros((LANES, LANES), jnp.bfloat16)
    last = lax.fori_loop(0, blocks, step, nothing, unroll=32)
    toeplitz_ref[blocks * LANES :, :] = jnp.where(upper, nothing, last)


def lagged(padded_ref, parts, rows, reach, lags):
    seen = {}

    def piece(lag, m):
        back, part = divmod(m - lag, parts)
        if (back, part) not in seen:
            rows_at = padded_ref[part, pl.ds(reach + back, rows), :]
            seen[back, part] = rows_at.astype(jnp.bfloat16)
        return seen[back, part]

    columns = [jnp.concatenate([piece(b, m) for m in range(parts)], axis=0) for b in lags]
    return jnp.concatenate(columns, axis=1) if len(columns) > 1 else columns[0]


def conv_channel(padded_ref, toeplitz_ref, parts, rows, reach, blocks, row_of=None, next_ref=None):
    total = jnp.zeros((parts * rows, LANES), jnp.float32)
    if next_ref is not None:
        upper = upper_mask()
        nothing = before = jnp.zeros((LANES, LANES), jnp.bfloat16)
    for start in range(0, blocks + 1, GROUP):
        lags = range(start, min(start + GROUP, blocks + 1))
        total = total + jnp.dot(
            lagged(padded_ref, parts, rows, reach, lags),
            toeplitz_ref[start * LANES : (lags[-1] + 1) * LANES, :],
            preferred_element_type=jnp.float32,
        )
        if next_ref is not None:
            for b in lags:
                if b < blocks:
                    before, block = toeplitz_block(row_of(b), before, upper)
                else:
                    block = jnp.where(upper, nothing, before)
                next_ref[b * LANES : (b + 1) * LANES, :] = block
    return total


def halves_of(chans):
    return 2 if chans % 8 == 0 else 1


def exchanged(first, second, half):
    low = lax.broadcasted_iota(jnp.int32, first.shape, 1) < half
    return (
        jnp.where(low, first, pltpu.roll(second, half, 1)),
        jnp.where(low, pltpu.roll(first, half, 1), second),
    )


def whole_kernel(
    spans, toks, chans, parts, reach, blocks,
    gain_hbm, tokens_hbm, w_in_hbm, short_hbm, filter_hbm, gated_ref,
    gain_ref, tokens_ref, w_in_ref, short_ref, filter_ref, taps_ref,
    projected_ref, rim_ref, sent_ref, held_ref, flat_ref, padded_ref,
    toeplitz_refs, result_ref, back_ref, returned_ref,
    load_sem, rim_send, rim_recv, out_send, out_recv, back_send, back_recv,
):
    peers = spans * toks
    tok_rows = parts * LANES
    halves = halves_of(chans)
    group = chans // halves
    rows = parts * group
    span_at, tok_at = lax.axis_index("span"), lax.axis_index("tok")
    me = span_at * toks + tok_at
    my_group = tok_at * spans + span_at
    first_chan = span_at * chans
    chan_offset = lax.rem(first_chan, RIM)

    def shifted(at, by, size):
        moved = at + by
        return jnp.where(moved >= size, moved - size, moved)

    def each_peer(act):
        for j in range(1, toks):
            act(span_at, shifted(tok_at, j, toks))

        def step(i, carry):
            for j in range(toks):
                act(shifted(span_at, i, spans), shifted(tok_at, j, toks))
            return carry

        lax.fori_loop(1, spans, step, 0)

    loads = [
        pltpu.make_async_copy(source, target, load_sem.at[i])
        for i, (source, target) in enumerate(
            [
                (tokens_hbm, tokens_ref),
                (w_in_hbm, w_in_ref),
                (
                    filter_hbm.at[pl.ds(pl.multiple_of(first_chan - chan_offset, RIM), RIM)],
                    filter_ref,
                ),
                (short_hbm, short_ref),
                (gain_hbm, gain_ref),
            ]
        )
    ]
    for load in loads:
        load.start()
    barrier = pltpu.get_barrier_semaphore()
    each_peer(
        lambda span, tok: pl.semaphore_signal(
            barrier, inc=1, device_id=(span, tok), device_id_type=MESH
        )
    )

    def project(values):
        return jnp.dot(values, w_in_ref[...], preferred_element_type=jnp.float32).astype(
            jnp.bfloat16
        ).astype(jnp.float32)

    loads[0].wait()
    loads[1].wait()
    for m in range(parts):
        projected_ref[RIM + m * LANES : RIM + (m + 1) * LANES, :] = project(
            tokens_ref[m * LANES : (m + 1) * LANES, :]
        )
    loads[2].wait()
    for b in range(blocks):
        taps_ref[b] = filter_ref[:, b * LANES : (b + 1) * LANES].astype(jnp.float32)
    loads[3].wait()
    loads[4].wait()
    pl.semaphore_wait(barrier, peers - 1)

    follower = lax.rem(me + 1, peers)
    following = (lax.div(follower, toks), lax.rem(follower, toks))
    rim_copy = pltpu.make_async_remote_copy(
        src_ref=tokens_ref.at[pl.ds(tok_rows - RIM, RIM)],
        dst_ref=rim_ref,
        send_sem=rim_send,
        recv_sem=rim_recv,
        device_id=following,
        device_id_type=MESH,
    )
    rim_copy.start()

    def mix(m, part):
        columns = slice(part * D, (part + 1) * D)
        first = RIM + m * LANES
        return (
            short_ref[0:1, columns] * projected_ref[first : first + LANES, columns]
            + short_ref[1:2, columns] * projected_ref[first - 1 : first - 1 + LANES, columns]
            + short_ref[2:3, columns] * projected_ref[first - 2 : first - 2 + LANES, columns]
        )

    def turned_product(m):
        return (mix(m, 1) * mix(m, 2)).T.reshape(peers, chans, LANES)

    turned = [turned_product(m) for m in range(1, parts)]
    rim_copy.wait()
    projected_ref[:RIM, :] = jnp.where(me > 0, project(rim_ref[...]), 0.0)
    turned = [turned_product(0)] + turned
    if halves == 1:
        sent_ref[0] = jnp.concatenate(turned, axis=1).astype(jnp.bfloat16)
    else:
        mated = [exchanged(turned[m], turned[m + 1], group) for m in range(0, parts, 2)]
        for h in range(halves):
            sent_ref[h] = jnp.concatenate([pair[h] for pair in mated], axis=1).astype(
                jnp.bfloat16
            )

    def out_copy(h, span, tok):
        return pltpu.make_async_remote_copy(
            src_ref=sent_ref.at[h, tok * spans + span],
            dst_ref=held_ref.at[h, me],
            send_sem=out_send.at[h],
            recv_sem=out_recv.at[h],
            device_id=(span, tok),
            device_id_type=MESH,
        )

    def back_copy(h, span, tok):
        return pltpu.make_async_remote_copy(
            src_ref=back_ref.at[h, span * toks + tok],
            dst_ref=returned_ref.at[h, my_group],
            send_sem=back_send.at[h],
            recv_sem=back_recv.at[h],
            device_id=(span, tok),
            device_id_type=MESH,
        )

    def all_of(h, source, target, send_sem, recv_sem):
        return pltpu.make_async_remote_copy(
            src_ref=source.at[h, pl.ds(0, peers - 1)],
            dst_ref=target.at[h, pl.ds(0, peers - 1)],
            send_sem=send_sem.at[h],
            recv_sem=recv_sem.at[h],
            device_id=following,
            device_id_type=MESH,
        )

    for h in range(halves):
        each_peer(lambda span, tok: out_copy(h, span, tok).start())
        held_ref[h, me] = sent_ref[h, my_group]

    def row_of(at):
        return lambda b: taps_ref[b, pl.ds(chan_offset + at, 1), :]

    def build(c, carry):
        build_toeplitz(row_of(c), blocks, toeplitz_refs[0].at[c])
        return carry

    padded_ref[:, :, :reach, :] = jnp.zeros((group, parts, reach, LANES), jnp.float32)

    for h in range(halves):
        if h == 0:
            lax.fori_loop(0, group, build, 0)
        all_of(h, sent_ref, held_ref, out_send, out_recv).wait_recv()
        flat_ref[...] = held_ref[h].astype(jnp.float32).reshape(peers * rows, LANES)

        for c in range(group):
            for m in range(parts):
                padded_ref[c, m, reach:, :] = flat_ref[pl.ds(m * group + c, peers, stride=rows), :]

        def convolve(c, carry):
            at = h * group + c
            ahead = (row_of(at + group), toeplitz_refs[h + 1].at[c]) if h + 1 < halves else ()
            total = conv_channel(
                padded_ref.at[c], toeplitz_refs[h].at[c], parts, peers, reach, blocks, *ahead
            )
            gain = gain_ref[first_chan + at]
            for m in range(parts):
                result_ref[pl.ds(m * group + c, peers, stride=rows), :] = (
                    total[m * peers : (m + 1) * peers] + gain * padded_ref[c, m, reach:, :]
                )
            return carry

        lax.fori_loop(0, group, convolve, 0, unroll=min(2, group))
        back_ref[h] = result_ref[...].reshape(peers, rows, LANES).astype(jnp.bfloat16)
        each_peer(lambda span, tok: back_copy(h, span, tok).start())
        returned_ref[h, my_group] = back_ref[h, me]

    query = [mix(m, 0) for m in range(parts)]
    for h in range(halves):
        all_of(h, back_ref, returned_ref, back_send, back_recv).wait_recv()
    if halves == 1:
        whole = returned_ref[0].astype(jnp.float32)
        pieces = [whole[:, m * chans : (m + 1) * chans, :] for m in range(parts)]
    else:
        pieces = []
        for m in range(0, parts, 2):
            pair = slice(m * group, (m + 2) * group)
            pieces += exchanged(
                *[returned_ref[h, :, pair, :].astype(jnp.float32) for h in range(halves)], group
            )
    for m in range(parts):
        gated_ref[m * LANES : (m + 1) * LANES, :] = (
            query[m] * pieces[m].reshape(D, LANES).T
        ).astype(jnp.bfloat16)
    for h in range(halves):
        all_of(h, sent_ref, held_ref, out_send, out_recv).wait_send()
        all_of(h, back_ref, returned_ref, back_send, back_recv).wait_send()


def per_device(tokens, w_in, short_filter, long_filter, skip_gain, w_out):
    tok_rows = tokens.shape[0]
    spans, toks = lax.axis_size("span"), lax.axis_size("tok")
    peers = spans * toks
    parts = tok_rows // LANES
    taps_count = long_filter.shape[1]
    blocks = taps_count // LANES
    reach = -(-taps_count // tok_rows)
    chans = long_filter.shape[0] // spans
    halves = halves_of(chans)
    rows = parts * chans // halves
    piece = (halves, peers, rows, LANES)
    flat = (peers * rows, LANES)
    gated_rows = pl.pallas_call(
        functools.partial(whole_kernel, spans, toks, chans, parts, reach, blocks),
        in_specs=[pl.BlockSpec(memory_space=pltpu.HBM)] * 5,
        out_specs=pl.BlockSpec(memory_space=pltpu.VMEM),
        out_shape=jax.ShapeDtypeStruct((tok_rows, D), jnp.bfloat16),
        scratch_shapes=[
            pltpu.SMEM(skip_gain.shape, skip_gain.dtype),
            pltpu.VMEM(tokens.shape, tokens.dtype),
            pltpu.VMEM(w_in.shape, w_in.dtype),
            pltpu.VMEM(short_filter.shape, short_filter.dtype),
            pltpu.VMEM((RIM, taps_count), long_filter.dtype),
            pltpu.VMEM((blocks, RIM, LANES), jnp.float32),
            pltpu.VMEM((RIM + tok_rows, 3 * D), jnp.float32),
            pltpu.VMEM((RIM, D), jnp.bfloat16),
            pltpu.VMEM(piece, jnp.bfloat16),
            pltpu.VMEM(piece, jnp.bfloat16),
            pltpu.VMEM(flat, jnp.float32),
            pltpu.VMEM((chans // halves, parts, reach + peers, LANES), jnp.float32),
            [pltpu.VMEM((chans // halves, (blocks + 1) * LANES, LANES), jnp.bfloat16)] * halves,
            pltpu.VMEM(flat, jnp.float32),
            pltpu.VMEM(piece, jnp.bfloat16),
            pltpu.VMEM(piece, jnp.bfloat16),
            pltpu.SemaphoreType.DMA((5,)),
            pltpu.SemaphoreType.DMA,
            pltpu.SemaphoreType.DMA,
            pltpu.SemaphoreType.DMA((halves,)),
            pltpu.SemaphoreType.DMA((halves,)),
            pltpu.SemaphoreType.DMA((halves,)),
            pltpu.SemaphoreType.DMA((halves,)),
        ],
        compiler_params=pltpu.CompilerParams(
            collective_id=0, has_side_effects=True, vmem_limit_bytes=60 * 1024 * 1024
        ),
    )(skip_gain, tokens, w_in, short_filter, long_filter)
    return jnp.dot(gated_rows, w_out, preferred_element_type=jnp.float32).astype(jnp.bfloat16)


def solution(mesh):
    return jax.shard_map(
        per_device,
        mesh=mesh,
        in_specs=(P(("span", "tok"), None), P(), P(), P("tok", None), P("tok"), P()),
        out_specs=P(("span", "tok"), None),
        check_vma=False,
    )
```

```python
import functools

import jax
import jax.numpy as jnp
from jax import lax
from jax.experimental import pallas as pl
from jax.experimental.pallas import tpu as pltpu
from jax.sharding import PartitionSpec as P

D = 256
LANES = 128
GROUP = 16
BAND = 16
RIM = 16
MESH = pl.DeviceIdType.MESH


def upper_mask():
    row_at = lax.broadcasted_iota(jnp.int32, (LANES, LANES), 0)
    col_at = lax.broadcasted_iota(jnp.int32, (LANES, LANES), 1)
    return (col_at - row_at).astype(jnp.int16) >= 0


def toeplitz_block(row, before, upper):
    spread = jnp.broadcast_to(row, (BAND, LANES))
    band = pltpu.roll(spread, 0, 1, stride=1, stride_axis=0).astype(jnp.bfloat16)
    turned = jnp.concatenate(
        [band] + [pltpu.roll(band, i, 1) for i in range(BAND, LANES, BAND)], axis=0
    )
    return turned, jnp.where(upper, turned, before)


def build_toeplitz(row_of, blocks, toeplitz_ref):
    upper = upper_mask()

    def step(b, before):
        turned, block = toeplitz_block(row_of(b), before, upper)
        toeplitz_ref[pl.ds(pl.multiple_of(b * LANES, LANES), LANES), :] = block
        return turned

    nothing = jnp.zeros((LANES, LANES), jnp.bfloat16)
    last = lax.fori_loop(0, blocks, step, nothing, unroll=8)
    toeplitz_ref[blocks * LANES :, :] = jnp.where(upper, nothing, last)


def lagged(padded_ref, parts, rows, reach, lags):
    seen = {}

    def piece(lag, m):
        back, part = divmod(m - lag, parts)
        if (back, part) not in seen:
            rows_at = padded_ref[part, pl.ds(reach + back, rows), :]
            seen[back, part] = rows_at.astype(jnp.bfloat16)
        return seen[back, part]

    columns = [jnp.concatenate([piece(b, m) for m in range(parts)], axis=0) for b in lags]
    return jnp.concatenate(columns, axis=1) if len(columns) > 1 else columns[0]


def conv_channel(padded_ref, toeplitz_ref, parts, rows, reach, blocks, row_of=None, next_ref=None):
    total = jnp.zeros((parts * rows, LANES), jnp.float32)
    if next_ref is not None:
        upper = upper_mask()
        nothing = before = jnp.zeros((LANES, LANES), jnp.bfloat16)
    for start in range(0, blocks + 1, GROUP):
        lags = range(start, min(start + GROUP, blocks + 1))
        total = total + jnp.dot(
            lagged(padded_ref, parts, rows, reach, lags),
            toeplitz_ref[start * LANES : (lags[-1] + 1) * LANES, :],
            preferred_element_type=jnp.float32,
        )
        if next_ref is not None:
            for b in lags:
                if b < blocks:
                    before, block = toeplitz_block(row_of(b), before, upper)
                else:
                    block = jnp.where(upper, nothing, before)
                next_ref[b * LANES : (b + 1) * LANES, :] = block
    return total


def halves_of(chans):
    return 2 if chans % 8 == 0 else 1


def exchanged(first, second, half):
    low = lax.broadcasted_iota(jnp.int32, first.shape, 1) < half
    return (
        jnp.where(low, first, pltpu.roll(second, half, 1)),
        jnp.where(low, pltpu.roll(first, half, 1), second),
    )


def whole_kernel(
    spans, toks, chans, parts, reach, blocks,
    gain_hbm, tokens_hbm, w_in_hbm, short_hbm, filter_hbm, w_out_hbm, out_ref,
    gain_ref, tokens_ref, w_in_ref, short_ref, filter_ref, w_out_ref, taps_ref,
    projected_ref, rim_ref, sent_ref, held_ref, flat_ref, padded_ref,
    toeplitz_refs, result_ref, back_ref, returned_ref,
    load_sem, rim_send, rim_recv, out_send, out_recv, back_send, back_recv,
):
    peers = spans * toks
    tok_rows = parts * LANES
    halves = halves_of(chans)
    group = chans // halves
    rows = parts * group
    span_at, tok_at = lax.axis_index("span"), lax.axis_index("tok")
    me = span_at * toks + tok_at
    my_group = tok_at * spans + span_at
    first_chan = span_at * chans
    chan_offset = lax.rem(first_chan, RIM)

    def shifted(at, by, size):
        moved = at + by
        return jnp.where(moved >= size, moved - size, moved)

    def each_peer(act):
        for j in range(1, toks):
            act(span_at, shifted(tok_at, j, toks))

        def step(i, carry):
            for j in range(toks):
                act(shifted(span_at, i, spans), shifted(tok_at, j, toks))
            return carry

        lax.fori_loop(1, spans, step, 0)

    loads = [
        pltpu.make_async_copy(source, target, load_sem.at[i])
        for i, (source, target) in enumerate(
            [
                (tokens_hbm, tokens_ref),
                (w_in_hbm, w_in_ref),
                (
                    filter_hbm.at[pl.ds(pl.multiple_of(first_chan - chan_offset, RIM), RIM)],
                    filter_ref,
                ),
                (short_hbm, short_ref),
                (w_out_hbm, w_out_ref),
                (gain_hbm, gain_ref),
            ]
        )
    ]
    for load in loads:
        load.start()
    barrier = pltpu.get_barrier_semaphore()
    each_peer(
        lambda span, tok: pl.semaphore_signal(
            barrier, inc=1, device_id=(span, tok), device_id_type=MESH
        )
    )

    def project(values):
        return jnp.dot(values, w_in_ref[...], preferred_element_type=jnp.float32).astype(
            jnp.bfloat16
        ).astype(jnp.float32)

    loads[0].wait()
    loads[1].wait()
    for m in range(parts):
        projected_ref[RIM + m * LANES : RIM + (m + 1) * LANES, :] = project(
            tokens_ref[m * LANES : (m + 1) * LANES, :]
        )
    loads[2].wait()
    for b in range(blocks):
        taps_ref[b] = filter_ref[:, b * LANES : (b + 1) * LANES].astype(jnp.float32)
    loads[3].wait()
    loads[4].wait()
    loads[5].wait()
    pl.semaphore_wait(barrier, peers - 1)

    follower = lax.rem(me + 1, peers)
    following = (lax.div(follower, toks), lax.rem(follower, toks))
    rim_copy = pltpu.make_async_remote_copy(
        src_ref=tokens_ref.at[pl.ds(tok_rows - RIM, RIM)],
        dst_ref=rim_ref,
        send_sem=rim_send,
        recv_sem=rim_recv,
        device_id=following,
        device_id_type=MESH,
    )
    rim_copy.start()

    def mix(m, part):
        columns = slice(part * D, (part + 1) * D)
        first = RIM + m * LANES
        return (
            short_ref[0:1, columns] * projected_ref[first : first + LANES, columns]
            + short_ref[1:2, columns] * projected_ref[first - 1 : first - 1 + LANES, columns]
            + short_ref[2:3, columns] * projected_ref[first - 2 : first - 2 + LANES, columns]
        )

    def turned_product(m):
        return (mix(m, 1) * mix(m, 2)).T.reshape(peers, chans, LANES)

    turned = [turned_product(m) for m in range(1, parts)]
    rim_copy.wait()
    projected_ref[:RIM, :] = jnp.where(me > 0, project(rim_ref[...]), 0.0)
    turned = [turned_product(0)] + turned
    if halves == 1:
        sent_ref[0] = jnp.concatenate(turned, axis=1).astype(jnp.bfloat16)
    else:
        mated = [exchanged(turned[m], turned[m + 1], group) for m in range(0, parts, 2)]
        for h in range(halves):
            sent_ref[h] = jnp.concatenate([pair[h] for pair in mated], axis=1).astype(
                jnp.bfloat16
            )

    def out_copy(h, span, tok):
        return pltpu.make_async_remote_copy(
            src_ref=sent_ref.at[h, tok * spans + span],
            dst_ref=held_ref.at[h, me],
            send_sem=out_send.at[h],
            recv_sem=out_recv.at[h],
            device_id=(span, tok),
            device_id_type=MESH,
        )

    def back_copy(h, span, tok):
        return pltpu.make_async_remote_copy(
            src_ref=back_ref.at[h, span * toks + tok],
            dst_ref=returned_ref.at[h, my_group],
            send_sem=back_send.at[h],
            recv_sem=back_recv.at[h],
            device_id=(span, tok),
            device_id_type=MESH,
        )

    def all_of(h, source, target, send_sem, recv_sem):
        return pltpu.make_async_remote_copy(
            src_ref=source.at[h, pl.ds(0, peers - 1)],
            dst_ref=target.at[h, pl.ds(0, peers - 1)],
            send_sem=send_sem.at[h],
            recv_sem=recv_sem.at[h],
            device_id=following,
            device_id_type=MESH,
        )

    for h in range(halves):
        each_peer(lambda span, tok: out_copy(h, span, tok).start())
        held_ref[h, me] = sent_ref[h, my_group]

    def row_of(at):
        return lambda b: taps_ref[b, pl.ds(chan_offset + at, 1), :]

    def build(c, carry):
        build_toeplitz(row_of(c), blocks, toeplitz_refs[0].at[c])
        return carry

    padded_ref[:, :reach, :] = jnp.zeros((parts, reach, LANES), jnp.float32)

    for h in range(halves):
        if h == 0:
            lax.fori_loop(0, group, build, 0)
        all_of(h, sent_ref, held_ref, out_send, out_recv).wait_recv()
        flat_ref[...] = held_ref[h].astype(jnp.float32).reshape(peers * rows, LANES)

        def convolve(c, carry):
            for m in range(parts):
                padded_ref[m, reach:, :] = flat_ref[pl.ds(m * group + c, peers, stride=rows), :]
            at = h * group + c
            ahead = (row_of(at + group), toeplitz_refs[h + 1].at[c]) if h + 1 < halves else ()
            total = conv_channel(
                padded_ref, toeplitz_refs[h].at[c], parts, peers, reach, blocks, *ahead
            )
            gain = gain_ref[first_chan + at]
            for m in range(parts):
                result_ref[pl.ds(m * group + c, peers, stride=rows), :] = (
                    total[m * peers : (m + 1) * peers] + gain * padded_ref[m, reach:, :]
                )
            return carry

        lax.fori_loop(0, group, convolve, 0)
        back_ref[h] = result_ref[...].reshape(peers, rows, LANES).astype(jnp.bfloat16)
        each_peer(lambda span, tok: back_copy(h, span, tok).start())
        returned_ref[h, my_group] = back_ref[h, me]

    query = [mix(m, 0) for m in range(parts)]
    for h in range(halves):
        all_of(h, back_ref, returned_ref, back_send, back_recv).wait_recv()
    if halves == 1:
        whole = returned_ref[0].astype(jnp.float32)
        pieces = [whole[:, m * chans : (m + 1) * chans, :] for m in range(parts)]
    else:
        pieces = []
        for m in range(0, parts, 2):
            pair = slice(m * group, (m + 2) * group)
            pieces += exchanged(
                *[returned_ref[h, :, pair, :].astype(jnp.float32) for h in range(halves)], group
            )
    for m in range(parts):
        gated = (query[m] * pieces[m].reshape(D, LANES).T).astype(jnp.bfloat16)
        out_ref[m * LANES : (m + 1) * LANES, :] = jnp.dot(
            gated, w_out_ref[...], preferred_element_type=jnp.float32
        ).astype(jnp.bfloat16)
    for h in range(halves):
        all_of(h, sent_ref, held_ref, out_send, out_recv).wait_send()
        all_of(h, back_ref, returned_ref, back_send, back_recv).wait_send()


def per_device(tokens, w_in, short_filter, long_filter, skip_gain, w_out):
    tok_rows = tokens.shape[0]
    spans, toks = lax.axis_size("span"), lax.axis_size("tok")
    peers = spans * toks
    parts = tok_rows // LANES
    taps_count = long_filter.shape[1]
    blocks = taps_count // LANES
    reach = -(-taps_count // tok_rows)
    chans = long_filter.shape[0] // spans
    halves = halves_of(chans)
    rows = parts * chans // halves
    piece = (halves, peers, rows, LANES)
    flat = (peers * rows, LANES)
    return pl.pallas_call(
        functools.partial(whole_kernel, spans, toks, chans, parts, reach, blocks),
        in_specs=[pl.BlockSpec(memory_space=pltpu.HBM)] * 6,
        out_specs=pl.BlockSpec(memory_space=pltpu.VMEM),
        out_shape=jax.ShapeDtypeStruct((tok_rows, D), jnp.bfloat16),
        scratch_shapes=[
            pltpu.SMEM(skip_gain.shape, skip_gain.dtype),
            pltpu.VMEM(tokens.shape, tokens.dtype),
            pltpu.VMEM(w_in.shape, w_in.dtype),
            pltpu.VMEM(short_filter.shape, short_filter.dtype),
            pltpu.VMEM((RIM, taps_count), long_filter.dtype),
            pltpu.VMEM(w_out.shape, w_out.dtype),
            pltpu.VMEM((blocks, RIM, LANES), jnp.float32),
            pltpu.VMEM((RIM + tok_rows, 3 * D), jnp.float32),
            pltpu.VMEM((RIM, D), jnp.bfloat16),
            pltpu.VMEM(piece, jnp.bfloat16),
            pltpu.VMEM(piece, jnp.bfloat16),
            pltpu.VMEM(flat, jnp.float32),
            pltpu.VMEM((parts, reach + peers, LANES), jnp.float32),
            [pltpu.VMEM((chans // halves, (blocks + 1) * LANES, LANES), jnp.bfloat16)] * halves,
            pltpu.VMEM(flat, jnp.float32),
            pltpu.VMEM(piece, jnp.bfloat16),
            pltpu.VMEM(piece, jnp.bfloat16),
            pltpu.SemaphoreType.DMA((6,)),
            pltpu.SemaphoreType.DMA,
            pltpu.SemaphoreType.DMA,
            pltpu.SemaphoreType.DMA((halves,)),
            pltpu.SemaphoreType.DMA((halves,)),
            pltpu.SemaphoreType.DMA((halves,)),
            pltpu.SemaphoreType.DMA((halves,)),
        ],
        compiler_params=pltpu.CompilerParams(
            collective_id=0, has_side_effects=True, vmem_limit_bytes=60 * 1024 * 1024
        ),
    )(skip_gain, tokens, w_in, short_filter, long_filter, w_out)


def solution(mesh):
    return jax.shard_map(
        per_device,
        mesh=mesh,
        in_specs=(P(("span", "tok"), None), P(), P(), P("tok", None), P("tok"), P()),
        out_specs=P(("span", "tok"), None),
        check_vma=False,
    )
```

```python
import functools

import jax
import jax.numpy as jnp
from jax import lax
from jax.experimental import pallas as pl
from jax.experimental.pallas import tpu as pltpu
from jax.sharding import PartitionSpec as P

D = 256
LANES = 128
GROUP = 8
BAND = 16
RIM = 16
MESH = pl.DeviceIdType.MESH


def upper_mask():
    row_at = lax.broadcasted_iota(jnp.int32, (LANES, LANES), 0)
    col_at = lax.broadcasted_iota(jnp.int32, (LANES, LANES), 1)
    return (col_at - row_at).astype(jnp.int16) >= 0


def toeplitz_block(row, before, upper):
    spread = jnp.broadcast_to(row, (BAND, LANES))
    band = pltpu.roll(spread, 0, 1, stride=1, stride_axis=0).astype(jnp.bfloat16)
    turned = jnp.concatenate(
        [band] + [pltpu.roll(band, i, 1) for i in range(BAND, LANES, BAND)], axis=0
    )
    return turned, jnp.where(upper, turned, before)


def build_toeplitz(row_of, blocks, toeplitz_ref):
    upper = upper_mask()

    def step(b, before):
        turned, block = toeplitz_block(row_of(b), before, upper)
        toeplitz_ref[pl.ds(pl.multiple_of(b * LANES, LANES), LANES), :] = block
        return turned

    nothing = jnp.zeros((LANES, LANES), jnp.bfloat16)
    last = lax.fori_loop(0, blocks, step, nothing, unroll=8)
    toeplitz_ref[blocks * LANES :, :] = jnp.where(upper, nothing, last)


def lagged(padded_ref, parts, rows, reach, lags):
    seen = {}

    def piece(lag, m):
        back, part = divmod(m - lag, parts)
        if (back, part) not in seen:
            rows_at = padded_ref[part, pl.ds(reach + back, rows), :]
            seen[back, part] = rows_at.astype(jnp.bfloat16)
        return seen[back, part]

    columns = [jnp.concatenate([piece(b, m) for m in range(parts)], axis=0) for b in lags]
    return jnp.concatenate(columns, axis=1) if len(columns) > 1 else columns[0]


def conv_channel(padded_ref, toeplitz_ref, parts, rows, reach, blocks, row_of=None, next_ref=None):
    total = jnp.zeros((parts * rows, LANES), jnp.float32)
    if next_ref is not None:
        upper = upper_mask()
        nothing = before = jnp.zeros((LANES, LANES), jnp.bfloat16)
    for start in range(0, blocks + 1, GROUP):
        lags = range(start, min(start + GROUP, blocks + 1))
        total = total + jnp.dot(
            lagged(padded_ref, parts, rows, reach, lags),
            toeplitz_ref[start * LANES : (lags[-1] + 1) * LANES, :],
            preferred_element_type=jnp.float32,
        )
        if next_ref is not None:
            for b in lags:
                if b < blocks:
                    before, block = toeplitz_block(row_of(b), before, upper)
                else:
                    block = jnp.where(upper, nothing, before)
                next_ref[b * LANES : (b + 1) * LANES, :] = block
    return total


def halves_of(chans):
    return 2 if chans % 8 == 0 else 1


def exchanged(first, second, half):
    low = lax.broadcasted_iota(jnp.int32, first.shape, 1) < half
    return (
        jnp.where(low, first, pltpu.roll(second, half, 1)),
        jnp.where(low, pltpu.roll(first, half, 1), second),
    )


def whole_kernel(
    spans, toks, chans, parts, reach, blocks,
    gain_hbm, tokens_hbm, w_in_hbm, short_hbm, filter_hbm, w_out_hbm, out_ref,
    gain_ref, tokens_ref, w_in_ref, short_ref, filter_ref, w_out_ref, taps_ref,
    projected_ref, rim_ref, sent_ref, held_ref, flat_ref, padded_ref,
    toeplitz_refs, result_ref, back_ref, returned_ref,
    load_sem, rim_send, rim_recv, out_send, out_recv, back_send, back_recv,
):
    peers = spans * toks
    tok_rows = parts * LANES
    halves = halves_of(chans)
    group = chans // halves
    rows = parts * group
    span_at, tok_at = lax.axis_index("span"), lax.axis_index("tok")
    me = span_at * toks + tok_at
    my_group = tok_at * spans + span_at
    first_chan = span_at * chans
    chan_offset = lax.rem(first_chan, RIM)

    def shifted(at, by, size):
        moved = at + by
        return jnp.where(moved >= size, moved - size, moved)

    def each_peer(act):
        for j in range(1, toks):
            act(span_at, shifted(tok_at, j, toks))

        def step(i, carry):
            for j in range(toks):
                act(shifted(span_at, i, spans), shifted(tok_at, j, toks))
            return carry

        lax.fori_loop(1, spans, step, 0)

    loads = [
        pltpu.make_async_copy(source, target, load_sem.at[i])
        for i, (source, target) in enumerate(
            [
                (tokens_hbm, tokens_ref),
                (w_in_hbm, w_in_ref),
                (
                    filter_hbm.at[pl.ds(pl.multiple_of(first_chan - chan_offset, RIM), RIM)],
                    filter_ref,
                ),
                (short_hbm, short_ref),
                (w_out_hbm, w_out_ref),
                (gain_hbm, gain_ref),
            ]
        )
    ]
    for load in loads:
        load.start()
    barrier = pltpu.get_barrier_semaphore()
    each_peer(
        lambda span, tok: pl.semaphore_signal(
            barrier, inc=1, device_id=(span, tok), device_id_type=MESH
        )
    )

    def project(values):
        return jnp.dot(values, w_in_ref[...], preferred_element_type=jnp.float32).astype(
            jnp.bfloat16
        ).astype(jnp.float32)

    loads[0].wait()
    loads[1].wait()
    for m in range(parts):
        projected_ref[RIM + m * LANES : RIM + (m + 1) * LANES, :] = project(
            tokens_ref[m * LANES : (m + 1) * LANES, :]
        )
    loads[2].wait()
    for b in range(blocks):
        taps_ref[b] = filter_ref[:, b * LANES : (b + 1) * LANES].astype(jnp.float32)
    loads[3].wait()
    loads[4].wait()
    loads[5].wait()
    pl.semaphore_wait(barrier, peers - 1)

    follower = lax.rem(me + 1, peers)
    following = (lax.div(follower, toks), lax.rem(follower, toks))
    rim_copy = pltpu.make_async_remote_copy(
        src_ref=tokens_ref.at[pl.ds(tok_rows - RIM, RIM)],
        dst_ref=rim_ref,
        send_sem=rim_send,
        recv_sem=rim_recv,
        device_id=following,
        device_id_type=MESH,
    )
    rim_copy.start()

    def mix(m, part):
        columns = slice(part * D, (part + 1) * D)
        first = RIM + m * LANES
        return (
            short_ref[0:1, columns] * projected_ref[first : first + LANES, columns]
            + short_ref[1:2, columns] * projected_ref[first - 1 : first - 1 + LANES, columns]
            + short_ref[2:3, columns] * projected_ref[first - 2 : first - 2 + LANES, columns]
        )

    def turned_product(m):
        return (mix(m, 1) * mix(m, 2)).T.reshape(peers, chans, LANES)

    turned = [turned_product(m) for m in range(1, parts)]
    rim_copy.wait()
    projected_ref[:RIM, :] = jnp.where(me > 0, project(rim_ref[...]), 0.0)
    turned = [turned_product(0)] + turned
    if halves == 1:
        sent_ref[0] = jnp.concatenate(turned, axis=1).astype(jnp.bfloat16)
    else:
        mated = [exchanged(turned[m], turned[m + 1], group) for m in range(0, parts, 2)]
        for h in range(halves):
            sent_ref[h] = jnp.concatenate([pair[h] for pair in mated], axis=1).astype(
                jnp.bfloat16
            )

    def out_copy(h, span, tok):
        return pltpu.make_async_remote_copy(
            src_ref=sent_ref.at[h, tok * spans + span],
            dst_ref=held_ref.at[h, me],
            send_sem=out_send.at[h],
            recv_sem=out_recv.at[h],
            device_id=(span, tok),
            device_id_type=MESH,
        )

    def back_copy(h, span, tok):
        return pltpu.make_async_remote_copy(
            src_ref=back_ref.at[h, span * toks + tok],
            dst_ref=returned_ref.at[h, my_group],
            send_sem=back_send.at[h],
            recv_sem=back_recv.at[h],
            device_id=(span, tok),
            device_id_type=MESH,
        )

    def all_of(h, source, target, send_sem, recv_sem):
        return pltpu.make_async_remote_copy(
            src_ref=source.at[h, pl.ds(0, peers - 1)],
            dst_ref=target.at[h, pl.ds(0, peers - 1)],
            send_sem=send_sem.at[h],
            recv_sem=recv_sem.at[h],
            device_id=following,
            device_id_type=MESH,
        )

    def send_out(h):
        each_peer(lambda span, tok: out_copy(h, span, tok).start())
        held_ref[h, me] = sent_ref[h, my_group]

    send_out(0)

    def row_of(at):
        return lambda b: taps_ref[b, pl.ds(chan_offset + at, 1), :]

    def build(c, carry):
        build_toeplitz(row_of(c), blocks, toeplitz_refs[0].at[c])
        return carry

    padded_ref[:, :reach, :] = jnp.zeros((parts, reach, LANES), jnp.float32)

    for h in range(halves):
        if h == 0:
            lax.fori_loop(0, group, build, 0)
            for later in range(1, halves):
                send_out(later)
        all_of(h, sent_ref, held_ref, out_send, out_recv).wait_recv()
        flat_ref[...] = held_ref[h].astype(jnp.float32).reshape(peers * rows, LANES)

        def convolve(c, carry):
            for m in range(parts):
                padded_ref[m, reach:, :] = flat_ref[pl.ds(m * group + c, peers, stride=rows), :]
            at = h * group + c
            ahead = (row_of(at + group), toeplitz_refs[h + 1].at[c]) if h + 1 < halves else ()
            total = conv_channel(
                padded_ref, toeplitz_refs[h].at[c], parts, peers, reach, blocks, *ahead
            )
            gain = gain_ref[first_chan + at]
            for m in range(parts):
                result_ref[pl.ds(m * group + c, peers, stride=rows), :] = (
                    total[m * peers : (m + 1) * peers] + gain * padded_ref[m, reach:, :]
                )
            return carry

        lax.fori_loop(0, group, convolve, 0)
        back_ref[h] = result_ref[...].reshape(peers, rows, LANES).astype(jnp.bfloat16)
        each_peer(lambda span, tok: back_copy(h, span, tok).start())
        returned_ref[h, my_group] = back_ref[h, me]

    query = [mix(m, 0) for m in range(parts)]
    for h in range(halves):
        all_of(h, back_ref, returned_ref, back_send, back_recv).wait_recv()
    if halves == 1:
        whole = returned_ref[0].astype(jnp.float32)
        pieces = [whole[:, m * chans : (m + 1) * chans, :] for m in range(parts)]
    else:
        pieces = []
        for m in range(0, parts, 2):
            pair = slice(m * group, (m + 2) * group)
            pieces += exchanged(
                *[returned_ref[h, :, pair, :].astype(jnp.float32) for h in range(halves)], group
            )
    for m in range(parts):
        gated = (query[m] * pieces[m].reshape(D, LANES).T).astype(jnp.bfloat16)
        out_ref[m * LANES : (m + 1) * LANES, :] = jnp.dot(
            gated, w_out_ref[...], preferred_element_type=jnp.float32
        ).astype(jnp.bfloat16)
    for h in range(halves):
        all_of(h, sent_ref, held_ref, out_send, out_recv).wait_send()
        all_of(h, back_ref, returned_ref, back_send, back_recv).wait_send()


def per_device(tokens, w_in, short_filter, long_filter, skip_gain, w_out):
    tok_rows = tokens.shape[0]
    spans, toks = lax.axis_size("span"), lax.axis_size("tok")
    peers = spans * toks
    parts = tok_rows // LANES
    taps_count = long_filter.shape[1]
    blocks = taps_count // LANES
    reach = -(-taps_count // tok_rows)
    chans = long_filter.shape[0] // spans
    halves = halves_of(chans)
    rows = parts * chans // halves
    piece = (halves, peers, rows, LANES)
    flat = (peers * rows, LANES)
    return pl.pallas_call(
        functools.partial(whole_kernel, spans, toks, chans, parts, reach, blocks),
        in_specs=[pl.BlockSpec(memory_space=pltpu.HBM)] * 6,
        out_specs=pl.BlockSpec(memory_space=pltpu.VMEM),
        out_shape=jax.ShapeDtypeStruct((tok_rows, D), jnp.bfloat16),
        scratch_shapes=[
            pltpu.SMEM(skip_gain.shape, skip_gain.dtype),
            pltpu.VMEM(tokens.shape, tokens.dtype),
            pltpu.VMEM(w_in.shape, w_in.dtype),
            pltpu.VMEM(short_filter.shape, short_filter.dtype),
            pltpu.VMEM((RIM, taps_count), long_filter.dtype),
            pltpu.VMEM(w_out.shape, w_out.dtype),
            pltpu.VMEM((blocks, RIM, LANES), jnp.float32),
            pltpu.VMEM((RIM + tok_rows, 3 * D), jnp.float32),
            pltpu.VMEM((RIM, D), jnp.bfloat16),
            pltpu.VMEM(piece, jnp.bfloat16),
            pltpu.VMEM(piece, jnp.bfloat16),
            pltpu.VMEM(flat, jnp.float32),
            pltpu.VMEM((parts, reach + peers, LANES), jnp.float32),
            [pltpu.VMEM((chans // halves, (blocks + 1) * LANES, LANES), jnp.bfloat16)] * halves,
            pltpu.VMEM(flat, jnp.float32),
            pltpu.VMEM(piece, jnp.bfloat16),
            pltpu.VMEM(piece, jnp.bfloat16),
            pltpu.SemaphoreType.DMA((6,)),
            pltpu.SemaphoreType.DMA,
            pltpu.SemaphoreType.DMA,
            pltpu.SemaphoreType.DMA((halves,)),
            pltpu.SemaphoreType.DMA((halves,)),
            pltpu.SemaphoreType.DMA((halves,)),
            pltpu.SemaphoreType.DMA((halves,)),
        ],
        compiler_params=pltpu.CompilerParams(
            collective_id=0, has_side_effects=True, vmem_limit_bytes=60 * 1024 * 1024
        ),
    )(skip_gain, tokens, w_in, short_filter, long_filter, w_out)


def solution(mesh):
    return jax.shard_map(
        per_device,
        mesh=mesh,
        in_specs=(P(("span", "tok"), None), P(), P(), P("tok", None), P("tok"), P()),
        out_specs=P(("span", "tok"), None),
        check_vma=False,
    )
```
